32 devices in a mesh: section: 4 (over z), rep: 4 (over y, core), tp: 2 (over x).
Axes of the slice: x: 2, y: 2, z: 4, core: 2. Of those that a mesh axis runs over, the one named last changes fastest.
Arguments:
- acts: bfloat16 [4, 256, 896], P('rep', None, 'tp'), may hold values from -6 to 6
- cotangent: bfloat16 [4, 256, 896], P('rep', None, 'tp'), may hold values from -8.5 to 8.5
- w_gate: bfloat16 [4, 4, 896, 4864], P('section', 'rep', None, 'tp'), may hold values from -3 to 3
- w_up: bfloat16 [4, 4, 896, 4864], P('section', 'rep', None, 'tp'), may hold values from -3 to 3
- w_down: bfloat16 [4, 4, 4864, 896], P('section', 'rep', 'tp'), may hold values from -4.2 to 4.2
- m_gate: bfloat16 [4, 4, 896, 4864], P('section', 'rep', None, 'tp'), may hold values from -0.099609375 to 0.099609375
- m_up: bfloat16 [4, 4, 896, 4864], P('section', 'rep', None, 'tp'), may hold values from -0.099609375 to 0.099609375
- m_down: bfloat16 [4, 4, 4864, 896], P('section', 'rep', 'tp'), may hold values from -0.099609375 to 0.099609375
- v_gate: bfloat16 [4, 4, 896, 4864], P('section', 'rep', None, 'tp'), may hold values from 0.0009994507 to 0.099609375
- v_up: bfloat16 [4, 4, 896, 4864], P('section', 'rep', None, 'tp'), may hold values from 0.0009994507 to 0.099609375
- v_down: bfloat16 [4, 4, 4864, 896], P('section', 'rep', 'tp'), may hold values from 0.0009994507 to 0.099609375
- steps: int32 [4], P('section'), may hold values from 0 to 999
Outputs:
- section_out: bfloat16 [4, 4, 256, 896], P('section', 'rep', None, 'tp')
- section_in_grad: bfloat16 [4, 4, 256, 896], P('section', 'rep', None, 'tp')
- new_gate: bfloat16 [4, 4, 896, 4864], P('section', 'rep', None, 'tp')
- new_up: bfloat16 [4, 4, 896, 4864], P('section', 'rep', None, 'tp')
- new_down: bfloat16 [4, 4, 4864, 896], P('section', 'rep', 'tp')
The draws below stay inside these ranges and needn't reach their ends.
All inputs are finite; a program needn't handle non-finite values.
Results may differ from the reference program's by a relative error of at most 0.023.
Values may be sent and summed in bfloat16 or wider, within the bound.
No kernel may reach another device: no remote copies, remote signals or barrier semaphores. Data moves between devices by JAX's collectives and lax.ppermute only.
A program may use at most 256 MiB of HBM per device.

```python
import math
import jax
import jax.numpy as jnp
from jax import lax

D = 896
FF = 4864
ROWS = 256
SECTIONS = 4
REPLICAS = 4
N_SECTION = 4
N_REP = 4


def noise_field(key, shape, bound):
    return jax.random.truncated_normal(key, -bound, bound, shape, jnp.float32)


def shared_acts(key):
    base = jax.random.fold_in(key, 11)
    shape = (REPLICAS, ROWS, D)
    values = noise_field(base, shape, 6.0)
    return values


def shared_up(key):
    base = jax.random.fold_in(key, 21)
    return noise_field(base, (SECTIONS, REPLICAS, D, FF), 3.0)


def draw_acts(key, part):
    return shared_acts(key).astype(jnp.bfloat16)


def draw_cotangent(key, part):
    common = shared_acts(key)
    extra = noise_field(jax.random.fold_in(key, 12), (REPLICAS, ROWS, D), 6.0)
    return (0.7 * common + 0.7 * extra).astype(jnp.bfloat16)


def draw_w_up(key, part):
    return shared_up(key).astype(jnp.bfloat16)


def draw_w_down(key, part):
    upper = shared_up(key)
    extra = noise_field(jax.random.fold_in(key, 22), (SECTIONS, REPLICAS, FF, D), 3.0)
    return (0.6 * jnp.swapaxes(upper, 2, 3) + 0.8 * extra).astype(jnp.bfloat16)


def touch_ends(entries, own_key, smallest, largest):
    place = [jax.random.randint(jax.random.fold_in(own_key, axis), (), 0, length) for axis, length in enumerate(entries.shape)]
    longest = entries.shape.index(max(entries.shape))
    next_to = place[:longest] + [(place[longest] + 1) % entries.shape[longest]] + place[longest + 1:]
    return entries.at[tuple(place)].set(smallest).at[tuple(next_to)].set(largest)


def block_levels(rng, shape, split, smallest, high):
    level = 1.0
    for axis_at, blocks in split:
        heights = jax.random.uniform(jax.random.fold_in(jax.random.fold_in(rng, 6), axis_at), (blocks,), jnp.float32, smallest / len(split), high / len(split))
        level = level * jnp.repeat(jnp.exp(heights), shape[axis_at] // blocks).reshape((-1,) + (1,) * (len(shape) - 1 - axis_at))
    return level


def gaussian(key, shape, scale, reach, split=(), held_as=jnp.bfloat16):
    array = scale * jax.random.normal(key, shape, jnp.float32)
    if split:
        array = array * block_levels(key, shape, split, -0.22, 0.18)
    return jnp.clip(array, -reach, reach).astype(held_as)


def setup_inputs(seed: int = 0) -> dict:
    key_of = jax.random.split(jax.random.key(seed), 13)
    return {
        "acts": draw_acts(jax.random.fold_in(key_of[12], 71), 0),
        "cotangent": draw_cotangent(jax.random.fold_in(key_of[12], 71), 0),
        "w_gate": gaussian(key_of[2], (SECTIONS, REPLICAS, D, FF), 1.0, 3.0, ((0, 4), (1, 4), (3, 2))),
        "w_up": draw_w_up(jax.random.fold_in(key_of[12], 71), 0),
        "w_down": draw_w_down(jax.random.fold_in(key_of[12], 71), 0),
        "m_gate": gaussian(key_of[5], (SECTIONS, REPLICAS, D, FF), 0.03, 0.099609375, ((0, 4), (1, 4), (3, 2))),
        "m_up": gaussian(key_of[6], (SECTIONS, REPLICAS, D, FF), 0.03, 0.099609375, ((0, 4), (1, 4), (3, 2))),
        "m_down": gaussian(key_of[7], (SECTIONS, REPLICAS, FF, D), 0.03, 0.099609375, ((0, 4), (1, 4), (2, 2))),
        "v_gate": jnp.clip(jnp.exp(math.log(0.099609375) - 4.6018058 * jax.random.uniform(key_of[8], (SECTIONS, REPLICAS, D, FF), jnp.float32) ** block_levels(key_of[8], (SECTIONS, REPLICAS, D, FF), ((0, 4), (1, 4), (3, 2)), -0.2, 0.2)), 0.0009994507, 0.099609375).astype(jnp.bfloat16),
        "v_up": jnp.clip(jnp.exp(math.log(0.099609375) - 4.6018058 * jax.random.uniform(key_of[9], (SECTIONS, REPLICAS, D, FF), jnp.float32) ** block_levels(key_of[9], (SECTIONS, REPLICAS, D, FF), ((0, 4), (1, 4), (3, 2)), -0.2, 0.2)), 0.0009994507, 0.099609375).astype(jnp.bfloat16),
        "v_down": jnp.clip(jnp.exp(math.log(0.099609375) - 4.6018058 * jax.random.uniform(key_of[10], (SECTIONS, REPLICAS, FF, D), jnp.float32) ** block_levels(key_of[10], (SECTIONS, REPLICAS, FF, D), ((0, 4), (1, 4), (2, 2)), -0.2, 0.2)), 0.0009994507, 0.099609375).astype(jnp.bfloat16),
        "steps": touch_ends(jax.random.randint(key_of[11], (SECTIONS,), 0, 1000), jax.random.fold_in(key_of[11], 1), 0, 999).astype(jnp.int32),
    }


NORM_EPS = 1e-06
ADAM_EPS = 1e-08
LEARN = 0.3
BETA_ONE = 0.9
BETA_TWO = 0.95

def forward_parts(x, wg, wu):
    xf = x.astype(jnp.float32)
    rms = jnp.sqrt(lax.optimization_barrier(jnp.mean(xf * xf, axis=1, keepdims=True)) + NORM_EPS)
    normed = xf / rms
    normed_b = normed.astype(jnp.bfloat16)
    gate = jnp.dot(normed_b, wg, preferred_element_type=jnp.float32) * (1.0 / math.sqrt(D))
    upper = jnp.dot(normed_b, wu, preferred_element_type=jnp.float32) * (1.0 / math.sqrt(D))
    return (xf, rms, normed, normed_b, gate, upper)

def adam_step(w, m, v, g):
    m_new = BETA_ONE * m.astype(jnp.float32) + (1.0 - BETA_ONE) * g
    v_new = BETA_TWO * v.astype(jnp.float32) + (1.0 - BETA_TWO) * g * g
    return (w.astype(jnp.float32) - LEARN * m_new / (jnp.sqrt(v_new) + ADAM_EPS)).astype(jnp.bfloat16)

def reference(acts, cotangent, w_gate, w_up, w_down, m_gate, m_up, m_down, v_gate, v_up, v_down, steps):
    outs_all = []
    grads_all = []
    gates_all = []
    ups_all = []
    downs_all = []
    for rep_idx in range(N_REP):
        inputs = []
        outputs = []
        x = acts[rep_idx]
        for section_idx in range(N_SECTION):
            inputs.append(x)
            xf, rms, normed, normed_b, gate, upper = forward_parts(x, w_gate[section_idx, rep_idx], w_up[section_idx, rep_idx])
            hidden = (jax.nn.silu(gate) * upper).astype(jnp.bfloat16)
            down = jnp.dot(hidden, w_down[section_idx, rep_idx], preferred_element_type=jnp.float32) * (1.0 / math.sqrt(FF))
            x = (xf + down).astype(jnp.bfloat16)
            outputs.append(x)
        in_grads = [None] * N_SECTION
        new_g = [None] * N_SECTION
        new_u = [None] * N_SECTION
        new_d = [None] * N_SECTION
        dy = cotangent[rep_idx]
        for section_idx in range(N_SECTION - 1, -1, -1):
            wg = w_gate[section_idx, rep_idx]
            wu = w_up[section_idx, rep_idx]
            wd = w_down[section_idx, rep_idx]
            xf, rms, normed, normed_b, gate, upper = forward_parts(inputs[section_idx], wg, wu)
            sig = jax.nn.sigmoid(gate)
            active = gate * sig
            hidden = (active * upper).astype(jnp.bfloat16)
            dh = jnp.dot(dy, wd.T, preferred_element_type=jnp.float32) * (1.0 / math.sqrt(FF))
            dgate = (dh * upper * sig * (1.0 + gate * (1.0 - sig))).astype(jnp.bfloat16)
            dup = (dh * active).astype(jnp.bfloat16)
            g_down = jnp.dot(hidden.T, dy, preferred_element_type=jnp.float32) * (1.0 / math.sqrt(FF))
            g_gate = jnp.dot(normed_b.T, dgate, preferred_element_type=jnp.float32) * (1.0 / math.sqrt(D))
            g_up = jnp.dot(normed_b.T, dup, preferred_element_type=jnp.float32) * (1.0 / math.sqrt(D))
            dnorm = (jnp.dot(dgate, wg.T, preferred_element_type=jnp.float32) + jnp.dot(dup, wu.T, preferred_element_type=jnp.float32)) * (1.0 / math.sqrt(D))
            stat = lax.optimization_barrier(jnp.sum(dnorm * normed, axis=1, keepdims=True)) / D
            dx = (dy.astype(jnp.float32) + (dnorm - normed * stat) / rms).astype(jnp.bfloat16)
            in_grads[section_idx] = dx
            new_g[section_idx] = adam_step(wg, m_gate[section_idx, rep_idx], v_gate[section_idx, rep_idx], g_gate)
            new_u[section_idx] = adam_step(wu, m_up[section_idx, rep_idx], v_up[section_idx, rep_idx], g_up)
            new_d[section_idx] = adam_step(wd, m_down[section_idx, rep_idx], v_down[section_idx, rep_idx], g_down)
            dy = dx
        outs_all.append(jnp.stack(outputs))
        grads_all.append(jnp.stack(in_grads))
        gates_all.append(jnp.stack(new_g))
        ups_all.append(jnp.stack(new_u))
        downs_all.append(jnp.stack(new_d))
    section_out = jnp.stack(outs_all, axis=1)
    section_in_grad = jnp.stack(grads_all, axis=1)
    updated = [jnp.stack(gates_all, axis=1), jnp.stack(ups_all, axis=1), jnp.stack(downs_all, axis=1)]
    levels = N_REP.bit_length() - 1
    results = []
    for weights in updated:
        rows = []
        for section_idx in range(N_SECTION):
            distance = jnp.left_shift(jnp.int32(1), (steps[section_idx] % levels).astype(jnp.int32))
            source = ((jnp.arange(N_REP, dtype=jnp.int32) - distance) % N_REP).astype(jnp.int32)
            partner = jnp.take(weights[section_idx], source, axis=0)
            rows.append(((weights[section_idx].astype(jnp.float32) + partner.astype(jnp.float32)) * 0.5).astype(jnp.bfloat16))
        results.append(jnp.stack(rows))
    return (section_out, section_in_grad, results[0], results[1], results[2])
```

```python
import math

import jax
import jax.numpy as jnp
from jax import lax
from jax.sharding import PartitionSpec as P

MB = 2
PARTS = {"down": 4, "gate": 4, "up": 4}

NORM_EPS = 1e-06
ADAM_EPS = 1e-08
LEARN = 0.3
BETA_ONE = 0.9
BETA_TWO = 0.95


def contract(left, right, left_dim, right_dim):
    return lax.dot_general(
        left, right, (((left_dim,), (right_dim,)), ((), ())), preferred_element_type=jnp.float32
    )


def tp_total(partial):
    own = partial.astype(jnp.bfloat16)
    peers = lax.axis_size("tp")
    if peers == 2:
        other = lax.ppermute(own, "tp", [(0, 1), (1, 0)])
        return own.astype(jnp.float32) + other.astype(jnp.float32)
    shares = lax.all_gather(own, "tp")
    return jnp.sum(shares.astype(jnp.float32), axis=0)


def handed_over(value, source, target):
    moved = lax.ppermute(value, "section", [(source, target)])
    return moved, lax.axis_index("section") == target


def norm_parts(x_full):
    xf = x_full.astype(jnp.float32)
    rms = jnp.sqrt(jnp.mean(xf * xf, axis=1, keepdims=True) + NORM_EPS)
    normed = xf / rms
    return xf, rms, normed, normed.astype(jnp.bfloat16)


def adam_step(weight, first, second, grad):
    m_new = BETA_ONE * first.astype(jnp.float32) + (1.0 - BETA_ONE) * grad
    v_new = BETA_TWO * second.astype(jnp.float32) + (1.0 - BETA_TWO) * grad * grad
    return (weight.astype(jnp.float32) - LEARN * m_new / (jnp.sqrt(v_new) + ADAM_EPS)).astype(
        jnp.bfloat16
    )


def partner_weights(own, which):
    peers = lax.axis_size("rep")
    levels = peers.bit_length() - 1

    def behind(value, by):
        return lax.ppermute(value, "rep", [(i, (i + by) % peers) for i in range(peers)])

    if levels == 1:
        return behind(own, 1)
    if levels > 2:
        return lax.switch(which, [lambda v, by=2**l: behind(v, by) for l in range(levels)], own)
    pair = lax.ppermute(own, "rep", [(i, i ^ 1) for i in range(peers)])
    near = which == 0
    far = behind(jnp.where(near, pair, own), 2)
    odd = lax.axis_index("rep") % 2 == 1
    return jnp.where(near & odd, pair, far)


def on_device(
    acts, cotangent, w_gate, w_up, w_down, m_gate, m_up, m_down, v_gate, v_up, v_down, steps
):
    sections = lax.axis_size("section")
    part = lax.axis_index("tp")
    rows, local_width = acts.shape[1:]
    wg, wu, wd = w_gate[0, 0], w_up[0, 0], w_down[0, 0]
    width, local_hidden = wg.shape
    hidden_units = local_hidden * lax.axis_size("tp")
    inv_d = 1.0 / math.sqrt(width)
    inv_ff = 1.0 / math.sqrt(hidden_units)
    tok = rows // MB

    x_all = lax.all_gather(acts[0], "tp", axis=1, tiled=True)
    dy_all = lax.all_gather(cotangent[0], "tp", axis=1, tiled=True)
    xs = [x_all[i * tok : (i + 1) * tok] for i in range(MB)]
    dys = [dy_all[i * tok : (i + 1) * tok] for i in range(MB)]

    kept = [None] * MB
    outs = [None] * MB
    for tick in range(sections):
        for i in range(MB):
            xf, rms, normed, normed_b = norm_parts(xs[i])
            gate = contract(normed_b, wg, 1, 0) * inv_d
            upper = contract(normed_b, wu, 1, 0) * inv_d
            sig = jax.nn.sigmoid(gate)
            active = gate * sig
            hidden = (active * upper).astype(jnp.bfloat16)
            share = contract(hidden, wd, 1, 0) * inv_ff
            y = (xf + tp_total(share)).astype(jnp.bfloat16)
            if tick < sections - 1:
                moved, takes = handed_over(y, tick, tick + 1)
                xs[i] = jnp.where(takes, moved, xs[i])
            else:
                slope = upper * sig * (1.0 + gate * (1.0 - sig))
                kept[i] = (rms, normed, normed_b, slope, active, hidden)
                outs[i] = y

    grads = [None] * MB
    dgates = [None] * MB
    dups = [None] * MB
    for tick in range(sections):
        for i in range(MB):
            rms, normed, normed_b, slope, active, hidden = kept[i]
            dh = contract(dys[i], wd, 1, 1) * inv_ff
            dgate = (dh * slope).astype(jnp.bfloat16)
            dup = (dh * active).astype(jnp.bfloat16)
            share = (contract(dgate, wg, 1, 1) + contract(dup, wu, 1, 1)) * inv_d
            dnorm = tp_total(share)
            stat = jnp.mean(dnorm * normed, axis=1, keepdims=True)
            dx = (dys[i].astype(jnp.float32) + (dnorm - normed * stat) / rms).astype(jnp.bfloat16)
            if tick < sections - 1:
                moved, takes = handed_over(dx, sections - 1 - tick, sections - 2 - tick)
                dys[i] = jnp.where(takes, moved, dys[i])
            else:
                grads[i], dgates[i], dups[i] = dx, dgate, dup

    normed_b = jnp.concatenate([k[2] for k in kept])
    hidden = jnp.concatenate([k[5] for k in kept])
    dy = jnp.concatenate(dys)
    dgate = jnp.concatenate(dgates)
    dup = jnp.concatenate(dups)
    which = steps[0] % (lax.axis_size("rep").bit_length() - 1)

    def renewed(weight, first, second, left, right, scale, parts):
        size = weight.shape[0] // parts
        done = []
        for p in range(parts):
            at = slice(p * size, (p + 1) * size)
            grad = contract(left[:, at], right, 0, 0) * scale
            own = adam_step(weight[at], first[at], second[at], grad)
            other = partner_weights(own, which)
            mean = (own.astype(jnp.float32) + other.astype(jnp.float32)) * 0.5
            done.append(mean.astype(jnp.bfloat16))
        return jnp.concatenate(done)[None, None]

    new_down = renewed(wd, m_down[0, 0], v_down[0, 0], hidden, dy, inv_ff, PARTS["down"])
    new_gate = renewed(wg, m_gate[0, 0], v_gate[0, 0], normed_b, dgate, inv_d, PARTS["gate"])
    new_up = renewed(wu, m_up[0, 0], v_up[0, 0], normed_b, dup, inv_d, PARTS["up"])

    def own_features(values):
        whole = jnp.concatenate(values)
        return lax.dynamic_slice_in_dim(whole, part * local_width, local_width, 1)[None, None]

    return own_features(outs), own_features(grads), new_gate, new_up, new_down


def solution(mesh):
    weights = P("section", "rep", None, "tp")
    rows_split = P("section", "rep", "tp", None)
    return jax.shard_map(
        on_device,
        mesh=mesh,
        in_specs=(
            P("rep", None, "tp"),
            P("rep", None, "tp"),
            weights,
            weights,
            rows_split,
            weights,
            weights,
            rows_split,
            weights,
            weights,
            rows_split,
            P("section"),
        ),
        out_specs=(weights, weights, weights, weights, rows_split),
        check_vma=False,
    )
```

```python
import math

import jax
import jax.numpy as jnp
from jax import lax
from jax.sharding import PartitionSpec as P

MB = 2
UNITS = 152
DOWN = (16, 40, 68, 96, 124, 152)
GATE = (38, 76, 114, 152)
UP = (38, 76, 114, 133, 152)
STREAMS = 2
AHEAD = 4


NORM_EPS = 1e-06
ADAM_EPS = 1e-08
LEARN = 0.3
BETA_ONE = 0.9
BETA_TWO = 0.95


def contract(left, right, left_dim, right_dim):
    return lax.dot_general(
        left, right, (((left_dim,), (right_dim,)), ((), ())), preferred_element_type=jnp.float32
    )


def tp_total(partial):
    own = partial.astype(jnp.bfloat16)
    peers = lax.axis_size("tp")
    if peers == 2:
        other = lax.ppermute(own, "tp", [(0, 1), (1, 0)])
        return own.astype(jnp.float32) + other.astype(jnp.float32)
    shares = lax.all_gather(own, "tp")
    return jnp.sum(shares.astype(jnp.float32), axis=0)


def all_features(local):
    if lax.axis_size("tp") == 2:
        other = lax.ppermute(local, "tp", [(0, 1), (1, 0)])
        first = lax.axis_index("tp") == 0
        return jnp.concatenate(
            [jnp.where(first, local, other), jnp.where(first, other, local)], axis=1
        )
    return lax.all_gather(local, "tp", axis=1, tiled=True)


def after(value, *earlier):
    return lax.optimization_barrier((value, *earlier))[0]


def handed_over(value, source, target):
    moved = lax.ppermute(value, "section", [(source, target)])
    return moved, lax.axis_index("section") == target


def norm_parts(x_full):
    xf = x_full.astype(jnp.float32)
    rms = jnp.sqrt(jnp.mean(xf * xf, axis=1, keepdims=True) + NORM_EPS)
    normed = xf / rms
    return xf, rms, normed, normed.astype(jnp.bfloat16)


def adam_step(weight, first, second, grad):
    m_new = BETA_ONE * first.astype(jnp.float32) + (1.0 - BETA_ONE) * grad
    v_new = BETA_TWO * second.astype(jnp.float32) + (1.0 - BETA_TWO) * grad * grad
    return (weight.astype(jnp.float32) - LEARN * m_new / (jnp.sqrt(v_new) + ADAM_EPS)).astype(
        jnp.bfloat16
    )


def from_below(value, by):
    peers = lax.axis_size("rep")
    return lax.ppermute(value, "rep", [(i, (i + by) % peers) for i in range(peers)])


def from_pair(value):
    return lax.ppermute(value, "rep", [(i, i ^ 1) for i in range(lax.axis_size("rep"))])


def partner_weights(own, which, pair_first, earlier):
    levels = lax.axis_size("rep").bit_length() - 1
    own_late = after(own, *earlier)
    if levels == 1:
        far = from_below(own_late, 1)
        return far, far
    if levels > 2:
        branches = [lambda v, by=2**l: from_below(v, by) for l in range(levels)]
        far = lax.switch(which, branches, own_late)
        return far, far
    near = which == 0
    odd = lax.axis_index("rep") % 2 == 1
    if pair_first:
        pair = from_pair(own)
        far = from_below(after(jnp.where(near, pair, own), *earlier), 2)
        return jnp.where(near & odd, pair, far), far
    far = from_below(own_late, 2)
    return jnp.where(near, from_pair(jnp.where(odd, far, own)), far), far


def on_device(
    acts, cotangent, w_gate, w_up, w_down, m_gate, m_up, m_down, v_gate, v_up, v_down, steps
):
    sections = lax.axis_size("section")
    part = lax.axis_index("tp")
    rows, local_width = acts.shape[1:]
    wg, wu, wd = w_gate[0, 0], w_up[0, 0], w_down[0, 0]
    width, local_hidden = wg.shape
    hidden_units = local_hidden * lax.axis_size("tp")
    inv_d = 1.0 / math.sqrt(width)
    inv_ff = 1.0 / math.sqrt(hidden_units)
    tok = rows // MB

    xs = [all_features(acts[0, i * tok : (i + 1) * tok]) for i in range(MB)]
    dy_all = all_features(after(cotangent[0], xs[-1]))
    dys = [dy_all[i * tok : (i + 1) * tok] for i in range(MB)]

    levels = lax.axis_size("rep").bit_length() - 1
    which = steps[0] % levels
    down_state = (wd, m_down[0, 0], v_down[0, 0])
    gate_state = (wg, m_gate[0, 0], v_gate[0, 0])
    up_state = (wu, m_up[0, 0], v_up[0, 0])
    kept = [None] * MB
    outs = [None] * MB
    for tick in range(sections):
        for i in range(MB):
            xf, rms, normed, normed_b = norm_parts(xs[i])
            gate = contract(normed_b, wg, 1, 0) * inv_d
            upper = contract(normed_b, wu, 1, 0) * inv_d
            sig = jax.nn.sigmoid(gate)
            active = gate * sig
            hidden = lax.optimization_barrier((active * upper).astype(jnp.bfloat16))
            share = contract(hidden, wd, 1, 0) * inv_ff
            y = (xf + tp_total(share)).astype(jnp.bfloat16)
            if tick < sections - 1:
                moved, takes = handed_over(y, tick, tick + 1)
                xs[i] = jnp.where(takes, moved, xs[i])
                dys[i] = after(dys[i], xs[i])
            else:
                slope = upper * sig * (1.0 + gate * (1.0 - sig))
                kept[i] = (rms, normed, normed_b, slope, active, hidden)
                outs[i] = y

    normed_all = jnp.concatenate([k[2] for k in kept])
    hidden_all = jnp.concatenate([k[5] for k in kept])
    sent = []

    def mean_of(own, other):
        return ((own.astype(jnp.float32) + other.astype(jnp.float32)) * 0.5).astype(jnp.bfloat16)

    def renewed(state, left, right, scale, parts):
        rows = state[0].shape[0]
        done, start = [], 0
        for upto in parts:
            size = rows * upto // UNITS - start
            at = slice(start, start + size)
            if len(sent) >= AHEAD:
                right = after(right, sent[-AHEAD])
            grad = contract(left[:, at], right, 0, 0) * scale
            own = adam_step(*(part[at] for part in state), grad)
            earlier = sent[-STREAMS:][:1] if len(sent) >= STREAMS else []
            other, far = partner_weights(own, which, state is up_state, earlier)
            sent.append(far)
            done.append((start, mean_of(own, other)))
            start += size
        return done

    def joined(shape, done):
        whole = jnp.zeros(shape, jnp.bfloat16)
        for start, mean in done:
            whole = lax.dynamic_update_slice(whole, mean, (start, 0))
        return whole

    grads = [None] * MB
    dgates = [None] * MB
    dups = [None] * MB
    for tick in range(sections):
        if tick == sections - 1:
            dy = jnp.concatenate(dys)
            down_done = renewed(down_state, hidden_all, dy, inv_ff, DOWN)
            dys = [after(value, far) for value, far in zip(dys, sent)]
        for i in range(MB):
            rms, normed, normed_b, slope, active, hidden = kept[i]
            dh = contract(dys[i], wd, 1, 1) * inv_ff
            dgate = (dh * slope).astype(jnp.bfloat16)
            dup = (dh * active).astype(jnp.bfloat16)
            share = (contract(dgate, wg, 1, 1) + contract(dup, wu, 1, 1)) * inv_d
            dnorm = tp_total(share)
            stat = jnp.mean(dnorm * normed, axis=1, keepdims=True)
            dx = (dys[i].astype(jnp.float32) + (dnorm - normed * stat) / rms).astype(jnp.bfloat16)
            if tick < sections - 1:
                moved, takes = handed_over(dx, sections - 1 - tick, sections - 2 - tick)
                dys[i] = jnp.where(takes, moved, dys[i])
            else:
                grads[i], dgates[i], dups[i] = dx, dgate, dup

    dgate = jnp.concatenate(dgates)
    dup = jnp.concatenate(dups)
    gate_done = renewed(gate_state, normed_all, dgate, inv_d, GATE)
    up_done = renewed(up_state, normed_all, dup, inv_d, UP)
    new_down = joined(wd.shape, down_done)
    new_gate = joined(wg.shape, gate_done)
    new_up = joined(wu.shape, up_done)

    def own_features(values):
        whole = jnp.concatenate(values)
        return lax.dynamic_slice_in_dim(whole, part * local_width, local_width, 1)[None, None]

    news = [new[None, None] for new in (new_gate, new_up, new_down)]
    return own_features(outs), own_features(grads), *news


def solution(mesh):
    weights = P("section", "rep", None, "tp")
    rows_split = P("section", "rep", "tp", None)
    return jax.shard_map(
        on_device,
        mesh=mesh,
        in_specs=(
            P("rep", None, "tp"),
            P("rep", None, "tp"),
            weights,
            weights,
            rows_split,
            weights,
            weights,
            rows_split,
            weights,
            weights,
            rows_split,
            P("section"),
        ),
        out_specs=(weights, weights, weights, weights, rows_split),
        check_vma=False,
    )
```

```python
import math

import jax
import jax.numpy as jnp
from jax import lax
from jax.experimental import pallas as pl
from jax.experimental.pallas import tpu as pltpu
from jax.sharding import PartitionSpec as P

MB = 2
UNITS = 152
DOWN = (76, 94, 126, 152)
GATE = (38, 76, 114, 152)
UP = (38, 76, 114, 133, 152)
STREAMS = 2
EARLY = 60
BLOCKS = 4
AHEAD = 4


NORM_EPS = 1e-06
ADAM_EPS = 1e-08
LEARN = 0.3
BETA_ONE = 0.9
BETA_TWO = 0.95


def contract(left, right, left_dim, right_dim):
    return lax.dot_general(
        left, right, (((left_dim,), (right_dim,)), ((), ())), preferred_element_type=jnp.float32
    )


def tp_total(partial):
    own = partial.astype(jnp.bfloat16)
    peers = lax.axis_size("tp")
    if peers == 2:
        other = lax.ppermute(own, "tp", [(0, 1), (1, 0)])
        return own.astype(jnp.float32) + other.astype(jnp.float32)
    shares = lax.all_gather(own, "tp")
    return jnp.sum(shares.astype(jnp.float32), axis=0)


def all_features(local):
    if lax.axis_size("tp") == 2:
        other = lax.ppermute(local, "tp", [(0, 1), (1, 0)])
        first = lax.axis_index("tp") == 0
        return jnp.concatenate(
            [jnp.where(first, local, other), jnp.where(first, other, local)], axis=1
        )
    return lax.all_gather(local, "tp", axis=1, tiled=True)


def after(value, *earlier):
    return lax.optimization_barrier((value, *earlier))[0]


def handed_over(value, source, target):
    moved = lax.ppermute(value, "section", [(source, target)])
    return moved, lax.axis_index("section") == target


def first_rows(arrays, rows):
    count = len(arrays)
    width = arrays[0].shape[1]
    size = rows // BLOCKS
    pieces = [(i, b * size) for i in range(count) for b in range(BLOCKS)]

    def kernel(*refs):
        held, landed, left = refs[-3:]
        out = refs[count]
        coming = [
            pltpu.make_async_copy(refs[i].at[pl.ds(at, size)], held.at[n], landed.at[n])
            for n, (i, at) in enumerate(pieces)
        ]
        going = [
            pltpu.make_async_copy(held.at[n], out.at[pl.ds(n * size, size)], left.at[n])
            for n in range(len(pieces))
        ]
        for copy in coming:
            copy.start()
        for come, go in zip(coming, going):
            come.wait()
            go.start()
        for copy in going:
            copy.wait()

    return pl.pallas_call(
        kernel,
        in_specs=[pl.BlockSpec(memory_space=pl.ANY)] * count,
        out_specs=pl.BlockSpec(memory_space=pl.ANY),
        out_shape=jax.ShapeDtypeStruct((count * rows, width), arrays[0].dtype),
        scratch_shapes=[
            pltpu.VMEM((len(pieces), size, width), arrays[0].dtype),
            pltpu.SemaphoreType.DMA((len(pieces),)),
            pltpu.SemaphoreType.DMA((len(pieces),)),
        ],
        compiler_params=pltpu.CompilerParams(vmem_limit_bytes=60 * 2**20),
        cost_estimate=pl.CostEstimate(
            flops=0, bytes_accessed=4 * count * rows * width, transcendentals=0
        ),
        name="first_rows",
    )(*arrays)


def norm_parts(x_full):
    xf = x_full.astype(jnp.float32)
    rms = jnp.sqrt(jnp.mean(xf * xf, axis=1, keepdims=True) + NORM_EPS)
    normed = xf / rms
    return xf, rms, normed, normed.astype(jnp.bfloat16)


def adam_step(weight, first, second, grad):
    m_new = BETA_ONE * first.astype(jnp.float32) + (1.0 - BETA_ONE) * grad
    v_new = BETA_TWO * second.astype(jnp.float32) + (1.0 - BETA_TWO) * grad * grad
    return (weight.astype(jnp.float32) - LEARN * m_new / (jnp.sqrt(v_new) + ADAM_EPS)).astype(
        jnp.bfloat16
    )


def from_below(value, by):
    peers = lax.axis_size("rep")
    return lax.ppermute(value, "rep", [(i, (i + by) % peers) for i in range(peers)])


def from_pair(value):
    return lax.ppermute(value, "rep", [(i, i ^ 1) for i in range(lax.axis_size("rep"))])


def partner_weights(own, which, pair_first, earlier):
    levels = lax.axis_size("rep").bit_length() - 1
    own_late = after(own, *earlier)
    if levels == 1:
        far = from_below(own_late, 1)
        return far, far
    if levels > 2:
        branches = [lambda v, by=2**l: from_below(v, by) for l in range(levels)]
        far = lax.switch(which, branches, own_late)
        return far, far
    near = which == 0
    odd = lax.axis_index("rep") % 2 == 1
    if pair_first:
        pair = from_pair(own)
        far = from_below(after(jnp.where(near, pair, own), *earlier), 2)
        return jnp.where(near & odd, pair, far), far
    far = from_below(own_late, 2)
    return jnp.where(near, from_pair(jnp.where(odd, far, own)), far), far


def on_device(
    acts, cotangent, w_gate, w_up, w_down, m_gate, m_up, m_down, v_gate, v_up, v_down, steps
):
    sections = lax.axis_size("section")
    part = lax.axis_index("tp")
    rows, local_width = acts.shape[1:]
    wg, wu, wd = w_gate[0, 0], w_up[0, 0], w_down[0, 0]
    width, local_hidden = wg.shape
    hidden_units = local_hidden * lax.axis_size("tp")
    inv_d = 1.0 / math.sqrt(width)
    inv_ff = 1.0 / math.sqrt(hidden_units)
    tok = rows // MB

    xs = [all_features(acts[0, i * tok : (i + 1) * tok]) for i in range(MB)]
    dy_all = all_features(after(cotangent[0], xs[-1]))
    dys = [dy_all[i * tok : (i + 1) * tok] for i in range(MB)]

    levels = lax.axis_size("rep").bit_length() - 1
    which = steps[0] % levels
    down_state = (wd, m_down[0, 0], v_down[0, 0])
    gate_state = (wg, m_gate[0, 0], v_gate[0, 0])
    up_state = (wu, m_up[0, 0], v_up[0, 0])
    early = local_hidden * EARLY // UNITS // (16 * BLOCKS) * 16 * BLOCKS if levels == 2 else 0
    if early:
        leaving = first_rows(down_state, early)
        far_state = from_below(leaving, 2)

    kept = [None] * MB
    outs = [None] * MB
    for tick in range(sections):
        for i in range(MB):
            xf, rms, normed, normed_b = norm_parts(xs[i])
            gate = contract(normed_b, wg, 1, 0) * inv_d
            upper = contract(normed_b, wu, 1, 0) * inv_d
            sig = jax.nn.sigmoid(gate)
            active = gate * sig
            hidden = lax.optimization_barrier((active * upper).astype(jnp.bfloat16))
            share = contract(hidden, wd, 1, 0) * inv_ff
            y = (xf + tp_total(share)).astype(jnp.bfloat16)
            if tick < sections - 1:
                moved, takes = handed_over(y, tick, tick + 1)
                xs[i] = jnp.where(takes, moved, xs[i])
                dys[i] = after(dys[i], xs[i])
            else:
                slope = upper * sig * (1.0 + gate * (1.0 - sig))
                kept[i] = (rms, normed, normed_b, slope, active, hidden)
                outs[i] = y

    normed_all = jnp.concatenate([k[2] for k in kept])
    hidden_all = jnp.concatenate([k[5] for k in kept])
    sent = []

    def mean_of(own, other):
        return ((own.astype(jnp.float32) + other.astype(jnp.float32)) * 0.5).astype(jnp.bfloat16)

    def renewed(state, left, right, scale, parts, start=0):
        rows = state[0].shape[0]
        done = []
        for upto in parts:
            size = rows * upto // UNITS - start
            if size <= 0:
                continue
            at = slice(start, start + size)
            if len(sent) >= AHEAD:
                right = after(right, sent[-AHEAD])
            grad = contract(left[:, at], right, 0, 0) * scale
            own = adam_step(*(part[at] for part in state), grad)
            earlier = sent[-STREAMS:][:1] if len(sent) >= STREAMS else []
            other, far = partner_weights(own, which, state is up_state, earlier)
            sent.append(far)
            done.append((start, mean_of(own, other)))
            start += size
        return done

    def joined(shape, done):
        whole = jnp.zeros(shape, jnp.bfloat16)
        for start, mean in done:
            whole = lax.dynamic_update_slice(whole, mean, (start, 0))
        return whole

    grads = [None] * MB
    dgates = [None] * MB
    dups = [None] * MB
    for tick in range(sections):
        if tick == sections - 2 and early:
            far_hidden = from_below(after(hidden_all[:, :early], dys[0]), 2)
        if tick == sections - 1:
            if early:
                dys[-1] = after(dys[-1], far_hidden)
            dy = jnp.concatenate(dys)
            if early:
                far_dy = [from_below(value, 2) for value in dys]
            down_done = renewed(down_state, hidden_all, dy, inv_ff, DOWN, early)
            dys = [after(value, far) for value, far in zip(dys, sent)]
        for i in range(MB):
            rms, normed, normed_b, slope, active, hidden = kept[i]
            dh = contract(dys[i], wd, 1, 1) * inv_ff
            dgate = (dh * slope).astype(jnp.bfloat16)
            dup = (dh * active).astype(jnp.bfloat16)
            share = (contract(dgate, wg, 1, 1) + contract(dup, wu, 1, 1)) * inv_d
            dnorm = tp_total(share)
            stat = jnp.mean(dnorm * normed, axis=1, keepdims=True)
            dx = (dys[i].astype(jnp.float32) + (dnorm - normed * stat) / rms).astype(jnp.bfloat16)
            if tick < sections - 1:
                moved, takes = handed_over(dx, sections - 1 - tick, sections - 2 - tick)
                dys[i] = jnp.where(takes, moved, dys[i])
            else:
                grads[i], dgates[i], dups[i] = dx, dgate, dup

    dgate = jnp.concatenate(dgates)
    dup = jnp.concatenate(dups)
    gate_done = renewed(gate_state, normed_all, dgate, inv_d, GATE)
    up_done = renewed(up_state, normed_all, dup, inv_d, UP)
    if early:
        far_dy = jnp.concatenate(far_dy)
        at = slice(0, early)
        grad = contract(hidden_all[:, at], after(dy, sent[-6]), 0, 0) * inv_ff
        own = adam_step(*(part[at] for part in down_state), grad)
        grad = contract(far_hidden, after(far_dy, sent[-4]), 0, 0) * inv_ff
        far = adam_step(*jnp.split(far_state, 3), grad)
        near = which == 0
        odd = lax.axis_index("rep") % 2 == 1
        other = jnp.where(near, from_pair(jnp.where(odd, far, own)), far)
        down_done.append((0, mean_of(own, other)))
    new_down = joined(wd.shape, down_done)
    new_gate = joined(wg.shape, gate_done)
    new_up = joined(wu.shape, up_done)

    def own_features(values):
        whole = jnp.concatenate(values)
        return lax.dynamic_slice_in_dim(whole, part * local_width, local_width, 1)[None, None]

    news = [new[None, None] for new in (new_gate, new_up, new_down)]
    return own_features(outs), own_features(grads), *news


def solution(mesh):
    weights = P("section", "rep", None, "tp")
    rows_split = P("section", "rep", "tp", None)
    return jax.shard_map(
        on_device,
        mesh=mesh,
        in_specs=(
            P("rep", None, "tp"),
            P("rep", None, "tp"),
            weights,
            weights,
            rows_split,
            weights,
            weights,
            rows_split,
            weights,
            weights,
            rows_split,
            P("section"),
        ),
        out_specs=(weights, weights, weights, weights, rows_split),
        check_vma=False,
    )
```

```python
import math

import jax
import jax.numpy as jnp
from jax import lax
from jax.experimental import pallas as pl
from jax.experimental.pallas import tpu as pltpu
from jax.sharding import PartitionSpec as P

MB = 2
UNITS = 152
DOWN = (76, 94, 126, 152)
GATE = (38, 76, 114, 152)
UP = (38, 76, 114, 133, 152)
STREAMS = 2
EARLY = 60
BLOCKS = 4
AHEAD = 4


NORM_EPS = 1e-06
ADAM_EPS = 1e-08
LEARN = 0.3
BETA_ONE = 0.9
BETA_TWO = 0.95


def contract(left, right, left_dim, right_dim):
    return lax.dot_general(
        left, right, (((left_dim,), (right_dim,)), ((), ())), preferred_element_type=jnp.float32
    )


def tp_total(partial):
    own = partial.astype(jnp.bfloat16)
    peers = lax.axis_size("tp")
    if peers == 2:
        other = lax.ppermute(own, "tp", [(0, 1), (1, 0)])
        return own.astype(jnp.float32) + other.astype(jnp.float32)
    shares = lax.all_gather(own, "tp")
    return jnp.sum(shares.astype(jnp.float32), axis=0)


def all_features(local):
    if lax.axis_size("tp") == 2:
        other = lax.ppermute(local, "tp", [(0, 1), (1, 0)])
        first = lax.axis_index("tp") == 0
        return jnp.concatenate(
            [jnp.where(first, local, other), jnp.where(first, other, local)], axis=1
        )
    return lax.all_gather(local, "tp", axis=1, tiled=True)


def after(value, *earlier):
    return lax.optimization_barrier((value, *earlier))[0]


def handed_over(value, source, target):
    moved = lax.ppermute(value, "section", [(source, target)])
    return moved, lax.axis_index("section") == target


def first_rows(arrays, rows):
    count = len(arrays)
    width = arrays[0].shape[1]
    size = rows // BLOCKS
    pieces = [(i, b * size) for i in range(count) for b in range(BLOCKS)]

    def kernel(*refs):
        held, landed, left = refs[-3:]
        out = refs[count]
        coming = [
            pltpu.make_async_copy(refs[i].at[pl.ds(at, size)], held.at[n], landed.at[n])
            for n, (i, at) in enumerate(pieces)
        ]
        going = [
            pltpu.make_async_copy(held.at[n], out.at[pl.ds(n * size, size)], left.at[n])
            for n in range(len(pieces))
        ]
        for copy in coming:
            copy.start()
        for come, go in zip(coming, going):
            come.wait()
            go.start()
        for copy in going:
            copy.wait()

    return pl.pallas_call(
        kernel,
        in_specs=[pl.BlockSpec(memory_space=pl.ANY)] * count,
        out_specs=pl.BlockSpec(memory_space=pl.ANY),
        out_shape=jax.ShapeDtypeStruct((count * rows, width), arrays[0].dtype),
        scratch_shapes=[
            pltpu.VMEM((len(pieces), size, width), arrays[0].dtype),
            pltpu.SemaphoreType.DMA((len(pieces),)),
            pltpu.SemaphoreType.DMA((len(pieces),)),
        ],
        compiler_params=pltpu.CompilerParams(vmem_limit_bytes=60 * 2**20),
        cost_estimate=pl.CostEstimate(
            flops=0, bytes_accessed=4 * count * rows * width, transcendentals=0
        ),
        name="first_rows",
    )(*arrays)


def norm_parts(x_full):
    xf = x_full.astype(jnp.float32)
    rms = jnp.sqrt(jnp.mean(xf * xf, axis=1, keepdims=True) + NORM_EPS)
    normed = xf / rms
    return xf, rms, normed, normed.astype(jnp.bfloat16)


def adam_step(weight, first, second, grad):
    m_new = BETA_ONE * first.astype(jnp.float32) + (1.0 - BETA_ONE) * grad
    v_new = BETA_TWO * second.astype(jnp.float32) + (1.0 - BETA_TWO) * grad * grad
    return (weight.astype(jnp.float32) - LEARN * m_new / (jnp.sqrt(v_new) + ADAM_EPS)).astype(
        jnp.bfloat16
    )


def from_below(value, by):
    peers = lax.axis_size("rep")
    return lax.ppermute(value, "rep", [(i, (i + by) % peers) for i in range(peers)])


def from_pair(value):
    return lax.ppermute(value, "rep", [(i, i ^ 1) for i in range(lax.axis_size("rep"))])


def partner_weights(own, which, pair_first, earlier):
    levels = lax.axis_size("rep").bit_length() - 1
    own_late = after(own, *earlier)
    if levels == 1:
        far = from_below(own_late, 1)
        return far, far
    if levels > 2:
        branches = [lambda v, by=2**l: from_below(v, by) for l in range(levels)]
        far = lax.switch(which, branches, own_late)
        return far, far
    near = which == 0
    odd = lax.axis_index("rep") % 2 == 1
    if pair_first:
        pair = from_pair(own)
        far = from_below(after(jnp.where(near, pair, own), *earlier), 2)
        return jnp.where(near & odd, pair, far), far
    far = from_below(own_late, 2)
    return jnp.where(near, from_pair(jnp.where(odd, far, own)), far), far


def on_device(
    acts, cotangent, w_gate, w_up, w_down, m_gate, m_up, m_down, v_gate, v_up, v_down, steps
):
    sections = lax.axis_size("section")
    part = lax.axis_index("tp")
    rows, local_width = acts.shape[1:]
    wg, wu, wd = w_gate[0, 0], w_up[0, 0], w_down[0, 0]
    width, local_hidden = wg.shape
    hidden_units = local_hidden * lax.axis_size("tp")
    inv_d = 1.0 / math.sqrt(width)
    inv_ff = 1.0 / math.sqrt(hidden_units)
    tok = rows // MB

    xs = [all_features(acts[0, i * tok : (i + 1) * tok]) for i in range(MB)]
    dy_all = all_features(after(cotangent[0], xs[-1]))
    dys = [dy_all[i * tok : (i + 1) * tok] for i in range(MB)]

    levels = lax.axis_size("rep").bit_length() - 1
    which = steps[0] % levels
    down_state = (wd, m_down[0, 0], v_down[0, 0])
    gate_state = (wg, m_gate[0, 0], v_gate[0, 0])
    up_state = (wu, m_up[0, 0], v_up[0, 0])
    early = local_hidden * EARLY // UNITS // (16 * BLOCKS) * 16 * BLOCKS if levels == 2 else 0
    if early:
        leaving = first_rows(down_state, early)
        far_state = from_below(leaving, 2)

    kept = [None] * MB
    outs = [None] * MB
    for tick in range(sections):
        for i in range(MB):
            xf, rms, normed, normed_b = norm_parts(xs[i])
            gate = contract(normed_b, wg, 1, 0) * inv_d
            upper = contract(normed_b, wu, 1, 0) * inv_d
            sig = jax.nn.sigmoid(gate)
            active = gate * sig
            hidden = lax.optimization_barrier((active * upper).astype(jnp.bfloat16))
            share = contract(hidden, wd, 1, 0) * inv_ff
            y = (xf + tp_total(share)).astype(jnp.bfloat16)
            if tick < sections - 1:
                moved, takes = handed_over(y, tick, tick + 1)
                xs[i] = jnp.where(takes, moved, xs[i])
                if tick < sections - 2:
                    dys[i] = after(dys[i], xs[i])
            else:
                slope = upper * sig * (1.0 + gate * (1.0 - sig))
                kept[i] = (rms, normed, normed_b, slope, active, hidden)
                outs[i] = y

    normed_all = jnp.concatenate([k[2] for k in kept])
    hidden_all = jnp.concatenate([k[5] for k in kept])
    sent = []

    def mean_of(own, other):
        return ((own.astype(jnp.float32) + other.astype(jnp.float32)) * 0.5).astype(jnp.bfloat16)

    def renewed(state, left, right, scale, parts, start=0):
        rows = state[0].shape[0]
        done = []
        for upto in parts:
            size = rows * upto // UNITS - start
            if size <= 0:
                continue
            at = slice(start, start + size)
            if len(sent) >= AHEAD:
                right = after(right, sent[-AHEAD])
            grad = contract(left[:, at], right, 0, 0) * scale
            own = adam_step(*(part[at] for part in state), grad)
            earlier = sent[-STREAMS:][:1] if len(sent) >= STREAMS else []
            other, far = partner_weights(own, which, state is up_state, earlier)
            sent.append(far)
            done.append((start, mean_of(own, other)))
            start += size
        return done

    def joined(shape, done):
        whole = jnp.zeros(shape, jnp.bfloat16)
        for start, mean in done:
            whole = lax.dynamic_update_slice(whole, mean, (start, 0))
        return whole

    grads = [None] * MB
    dgates = [None] * MB
    dups = [None] * MB
    for tick in range(sections):
        if tick == sections - 2 and early:
            far_hidden = from_below(after(hidden_all[:, :early], dys[0]), 2)
        if tick == sections - 1:
            if early:
                dys[-1] = after(dys[-1], far_hidden)
            dy = jnp.concatenate(dys)
            if early:
                far_dy = [from_below(value, 2) for value in dys]
            down_done = renewed(down_state, hidden_all, dy, inv_ff, DOWN, early)
            dys = [after(value, far) for value, far in zip(dys, sent)]
        for i in range(MB):
            rms, normed, normed_b, slope, active, hidden = kept[i]
            dh = contract(dys[i], wd, 1, 1) * inv_ff
            dgate = (dh * slope).astype(jnp.bfloat16)
            dup = (dh * active).astype(jnp.bfloat16)
            share = (contract(dgate, wg, 1, 1) + contract(dup, wu, 1, 1)) * inv_d
            dnorm = tp_total(share)
            stat = jnp.mean(dnorm * normed, axis=1, keepdims=True)
            dx = (dys[i].astype(jnp.float32) + (dnorm - normed * stat) / rms).astype(jnp.bfloat16)
            if tick < sections - 1:
                moved, takes = handed_over(dx, sections - 1 - tick, sections - 2 - tick)
                dys[i] = jnp.where(takes, moved, dys[i])
            else:
                grads[i], dgates[i], dups[i] = dx, dgate, dup

    dgate = jnp.concatenate(dgates)
    dup = jnp.concatenate(dups)
    gate_done = renewed(gate_state, normed_all, dgate, inv_d, GATE)
    up_done = renewed(up_state, normed_all, dup, inv_d, UP)
    if early:
        far_dy = jnp.concatenate(far_dy)
        at = slice(0, early)
        grad = contract(hidden_all[:, at], after(dy, sent[-6]), 0, 0) * inv_ff
        own = adam_step(*(part[at] for part in down_state), grad)
        grad = contract(far_hidden, after(far_dy, sent[-4]), 0, 0) * inv_ff
        far = adam_step(*jnp.split(far_state, 3), grad)
        near = which == 0
        odd = lax.axis_index("rep") % 2 == 1
        other = jnp.where(near, from_pair(jnp.where(odd, far, own)), far)
        down_done.append((0, mean_of(own, other)))
    new_down = joined(wd.shape, down_done)
    new_gate = joined(wg.shape, gate_done)
    new_up = joined(wu.shape, up_done)

    def own_features(values):
        whole = jnp.concatenate(values)
        return lax.dynamic_slice_in_dim(whole, part * local_width, local_width, 1)[None, None]

    news = [new[None, None] for new in (new_gate, new_up, new_down)]
    return own_features(outs), own_features(grads), *news


def solution(mesh):
    weights = P("section", "rep", None, "tp")
    rows_split = P("section", "rep", "tp", None)
    return jax.shard_map(
        on_device,
        mesh=mesh,
        in_specs=(
            P("rep", None, "tp"),
            P("rep", None, "tp"),
            weights,
            weights,
            rows_split,
            weights,
            weights,
            rows_split,
            weights,
            weights,
            rows_split,
            P("section"),
        ),
        out_specs=(weights, weights, weights, weights, rows_split),
        check_vma=False,
    )
```

```python
import math

import jax
import jax.numpy as jnp
from jax import lax
from jax.experimental import pallas as pl
from jax.experimental.pallas import tpu as pltpu
from jax.sharding import PartitionSpec as P

MB = 2
UNITS = 152
DOWN = (76, 94, 126, 152)
GATE = (38, 76, 114, 152)
UP = (38, 76, 114, 133, 152)
STREAMS = 2
EARLY = 60
BLOCKS = 4
AHEAD = 4


NORM_EPS = 1e-06
ADAM_EPS = 1e-08
LEARN = 0.3
BETA_ONE = 0.9
BETA_TWO = 0.95


def contract(left, right, left_dim, right_dim):
    return lax.dot_general(
        left, right, (((left_dim,), (right_dim,)), ((), ())), preferred_element_type=jnp.float32
    )


def tp_total(partial):
    own = partial.astype(jnp.bfloat16)
    peers = lax.axis_size("tp")
    if peers == 2:
        other = lax.ppermute(own, "tp", [(0, 1), (1, 0)])
        return own.astype(jnp.float32) + other.astype(jnp.float32)
    shares = lax.all_gather(own, "tp")
    return jnp.sum(shares.astype(jnp.float32), axis=0)


def all_features(local):
    if lax.axis_size("tp") == 2:
        other = lax.ppermute(local, "tp", [(0, 1), (1, 0)])
        first = lax.axis_index("tp") == 0
        return jnp.concatenate(
            [jnp.where(first, local, other), jnp.where(first, other, local)], axis=1
        )
    return lax.all_gather(local, "tp", axis=1, tiled=True)


def after(value, *earlier):
    return lax.optimization_barrier((value, *earlier))[0]


def handed_over(value, source, target):
    moved = lax.ppermute(value, "section", [(source, target)])
    return moved, lax.axis_index("section") == target


def first_rows(arrays, rows):
    count = len(arrays)
    width = arrays[0].shape[1]
    size = rows // BLOCKS
    pieces = [(i, b * size) for i in range(count) for b in range(BLOCKS)]

    def kernel(*refs):
        held, landed, left = refs[-3:]
        out = refs[count]
        coming = [
            pltpu.make_async_copy(refs[i].at[pl.ds(at, size)], held.at[n], landed.at[n])
            for n, (i, at) in enumerate(pieces)
        ]
        going = [
            pltpu.make_async_copy(held.at[n], out.at[pl.ds(n * size, size)], left.at[n])
            for n in range(len(pieces))
        ]
        for copy in coming:
            copy.start()
        for come, go in zip(coming, going):
            come.wait()
            go.start()
        for copy in going:
            copy.wait()

    return pl.pallas_call(
        kernel,
        in_specs=[pl.BlockSpec(memory_space=pl.ANY)] * count,
        out_specs=pl.BlockSpec(memory_space=pl.ANY),
        out_shape=jax.ShapeDtypeStruct((count * rows, width), arrays[0].dtype),
        scratch_shapes=[
            pltpu.VMEM((len(pieces), size, width), arrays[0].dtype),
            pltpu.SemaphoreType.DMA((len(pieces),)),
            pltpu.SemaphoreType.DMA((len(pieces),)),
        ],
        compiler_params=pltpu.CompilerParams(vmem_limit_bytes=60 * 2**20),
        cost_estimate=pl.CostEstimate(
            flops=0, bytes_accessed=4 * count * rows * width, transcendentals=0
        ),
        name="first_rows",
    )(*arrays)


def norm_parts(x_full):
    xf = x_full.astype(jnp.float32)
    rms = jnp.sqrt(jnp.mean(xf * xf, axis=1, keepdims=True) + NORM_EPS)
    normed = xf / rms
    return xf, rms, normed, normed.astype(jnp.bfloat16)


def adam_step(weight, first, second, grad):
    m_new = BETA_ONE * first.astype(jnp.float32) + (1.0 - BETA_ONE) * grad
    v_new = BETA_TWO * second.astype(jnp.float32) + (1.0 - BETA_TWO) * grad * grad
    return (weight.astype(jnp.float32) - LEARN * m_new / (jnp.sqrt(v_new) + ADAM_EPS)).astype(
        jnp.bfloat16
    )


def from_below(value, by):
    peers = lax.axis_size("rep")
    return lax.ppermute(value, "rep", [(i, (i + by) % peers) for i in range(peers)])


def from_pair(value):
    return lax.ppermute(value, "rep", [(i, i ^ 1) for i in range(lax.axis_size("rep"))])


def partner_weights(own, which, pair_first, earlier):
    levels = lax.axis_size("rep").bit_length() - 1
    own_late = after(own, *earlier)
    if levels == 1:
        far = from_below(own_late, 1)
        return far, far
    if levels > 2:
        branches = [lambda v, by=2**l: from_below(v, by) for l in range(levels)]
        far = lax.switch(which, branches, own_late)
        return far, far
    near = which == 0
    odd = lax.axis_index("rep") % 2 == 1
    if pair_first:
        pair = from_pair(own)
        far = from_below(after(jnp.where(near, pair, own), *earlier), 2)
        return jnp.where(near & odd, pair, far), far
    far = from_below(own_late, 2)
    return jnp.where(near, from_pair(jnp.where(odd, far, own)), far), far


def on_device(
    acts, cotangent, w_gate, w_up, w_down, m_gate, m_up, m_down, v_gate, v_up, v_down, steps
):
    sections = lax.axis_size("section")
    part = lax.axis_index("tp")
    rows, local_width = acts.shape[1:]
    wg, wu, wd = w_gate[0, 0], w_up[0, 0], w_down[0, 0]
    width, local_hidden = wg.shape
    hidden_units = local_hidden * lax.axis_size("tp")
    inv_d = 1.0 / math.sqrt(width)
    inv_ff = 1.0 / math.sqrt(hidden_units)
    tok = rows // MB

    xs = [all_features(acts[0, i * tok : (i + 1) * tok]) for i in range(MB)]
    dy_all = all_features(after(cotangent[0], xs[-1]))
    dys = [dy_all[i * tok : (i + 1) * tok] for i in range(MB)]

    levels = lax.axis_size("rep").bit_length() - 1
    which = steps[0] % levels
    down_state = (wd, m_down[0, 0], v_down[0, 0])
    gate_state = (wg, m_gate[0, 0], v_gate[0, 0])
    up_state = (wu, m_up[0, 0], v_up[0, 0])
    early = local_hidden * EARLY // UNITS // (16 * BLOCKS) * 16 * BLOCKS if levels == 2 else 0
    if early:
        leaving = first_rows(down_state, early)
        far_state = from_below(leaving, 2)

    kept = [None] * MB
    outs = [None] * MB
    for tick in range(sections):
        for i in range(MB):
            xf, rms, normed, normed_b = norm_parts(xs[i])
            gate = contract(normed_b, wg, 1, 0) * inv_d
            upper = contract(normed_b, wu, 1, 0) * inv_d
            sig = jax.nn.sigmoid(gate)
            active = gate * sig
            hidden = lax.optimization_barrier((active * upper).astype(jnp.bfloat16))
            share = contract(hidden, wd, 1, 0) * inv_ff
            y = (xf + tp_total(share)).astype(jnp.bfloat16)
            if tick < sections - 1:
                moved, takes = handed_over(y, tick, tick + 1)
                xs[i] = jnp.where(takes, moved, xs[i])
                if tick < sections - 2:
                    dys[i] = after(dys[i], xs[i])
            else:
                slope = upper * sig * (1.0 + gate * (1.0 - sig))
                kept[i] = (rms, normed, normed_b, slope, active, hidden)
                outs[i] = y

    normed_all = jnp.concatenate([k[2] for k in kept])
    hidden_all = jnp.concatenate([k[5] for k in kept])
    sent = []

    def mean_of(own, other):
        return ((own.astype(jnp.float32) + other.astype(jnp.float32)) * 0.5).astype(jnp.bfloat16)

    def renewed(state, left, right, scale, parts, start=0):
        rows = state[0].shape[0]
        done = []
        for upto in parts:
            size = rows * upto // UNITS - start
            if size <= 0:
                continue
            at = slice(start, start + size)
            if len(sent) >= AHEAD:
                right = after(right, sent[-AHEAD])
            grad = contract(left[:, at], right, 0, 0) * scale
            own = adam_step(*(part[at] for part in state), grad)
            earlier = sent[-STREAMS:][:1] if len(sent) >= STREAMS else []
            other, far = partner_weights(own, which, state is up_state and upto > UP[-3], earlier)
            sent.append(far)
            done.append((start, mean_of(own, other)))
            start += size
        return done

    def joined(shape, done):
        whole = jnp.zeros(shape, jnp.bfloat16)
        for start, mean in done:
            whole = lax.dynamic_update_slice(whole, mean, (start, 0))
        return whole

    grads = [None] * MB
    dgates = [None] * MB
    dups = [None] * MB
    for tick in range(sections):
        if tick == sections - 2 and early:
            far_hidden = from_below(after(hidden_all[:, :early], dys[0]), 2)
        if tick == sections - 1:
            if early:
                dys[-1] = after(dys[-1], far_hidden)
            dy = jnp.concatenate(dys)
            if early:
                far_dy = [from_below(value, 2) for value in dys]
            down_done = renewed(down_state, hidden_all, dy, inv_ff, DOWN, early)
            dys = [after(value, far) for value, far in zip(dys, sent)]
        for i in range(MB):
            rms, normed, normed_b, slope, active, hidden = kept[i]
            dh = contract(dys[i], wd, 1, 1) * inv_ff
            dgate = (dh * slope).astype(jnp.bfloat16)
            dup = (dh * active).astype(jnp.bfloat16)
            share = (contract(dgate, wg, 1, 1) + contract(dup, wu, 1, 1)) * inv_d
            dnorm = tp_total(share)
            stat = jnp.mean(dnorm * normed, axis=1, keepdims=True)
            dx = (dys[i].astype(jnp.float32) + (dnorm - normed * stat) / rms).astype(jnp.bfloat16)
            if tick < sections - 1:
                moved, takes = handed_over(dx, sections - 1 - tick, sections - 2 - tick)
                dys[i] = jnp.where(takes, moved, dys[i])
            else:
                grads[i], dgates[i], dups[i] = dx, dgate, dup

    dgate = jnp.concatenate(dgates)
    dup = jnp.concatenate(dups)
    gate_done = renewed(gate_state, normed_all, dgate, inv_d, GATE)
    up_done = renewed(up_state, normed_all, dup, inv_d, UP)
    if early:
        far_dy = jnp.concatenate(far_dy)
        at = slice(0, early)
        grad = contract(hidden_all[:, at], after(dy, sent[-6]), 0, 0) * inv_ff
        own = adam_step(*(part[at] for part in down_state), grad)
        grad = contract(far_hidden, after(far_dy, sent[-4]), 0, 0) * inv_ff
        far = adam_step(*jnp.split(far_state, 3), grad)
        near = which == 0
        odd = lax.axis_index("rep") % 2 == 1
        other = jnp.where(near, from_pair(jnp.where(odd, far, own)), far)
        down_done.append((0, mean_of(own, other)))
    new_down = joined(wd.shape, down_done)
    new_gate = joined(wg.shape, gate_done)
    new_up = joined(wu.shape, up_done)

    def own_features(values):
        whole = jnp.concatenate(values)
        return lax.dynamic_slice_in_dim(whole, part * local_width, local_width, 1)[None, None]

    news = [new[None, None] for new in (new_gate, new_up, new_down)]
    return own_features(outs), own_features(grads), *news


def solution(mesh):
    weights = P("section", "rep", None, "tp")
    rows_split = P("section", "rep", "tp", None)
    return jax.shard_map(
        on_device,
        mesh=mesh,
        in_specs=(
            P("rep", None, "tp"),
            P("rep", None, "tp"),
            weights,
            weights,
            rows_split,
            weights,
            weights,
            rows_split,
            weights,
            weights,
            rows_split,
            P("section"),
        ),
        out_specs=(weights, weights, weights, weights, rows_split),
        check_vma=False,
    )
```
